256 devices in a mesh: blk: 64 (over y, z, core), kv: 4 (over x).
Axes of the slice: x: 4, y: 4, z: 8, core: 2. Of those that a mesh axis runs over, the one named last changes fastest.
Arguments:
- queries: bfloat16 [32768, 3072], P(('blk', 'kv')), may hold values from -480 to 480
- latent: bfloat16 [32768, 576], P(('blk', 'kv')), may hold values from -6 to 6
- norm_gain: float32 [512], replicated, may hold values from 0.5 to 1.5
- kv_up: bfloat16 [512, 4096], replicated, may hold values from -0.5 to 0.5
- block_mask: int32 [64, 64], P('blk'), may hold values from 0 to 1, as said below
- positions: int32 [32768], P(('blk', 'kv')), may hold values from 0 to 32767
Outputs:
- attended: bfloat16 [32768, 2048], P(('blk', 'kv'))
The draws below stay inside these ranges and needn't reach their ends.
Inputs may be any that keep to these rules, and one draw needn't show every extreme that they name: block_mask[i][j] is 0 for j > i and 1 for j = i and j = i - 1; each row has at most 5 ones, and the last row has exactly 5.
All inputs are finite; a program needn't handle non-finite values.
Results may differ from the reference program's by a relative error of at most 0.017.
The reference program's roundings to bfloat16 on the way count: a program that leaves them out, or rounds other values in their place, can miss the bound.
Values may be sent and summed in bfloat16 or wider, within the bound.
A program may use at most 320 MiB of HBM per device.

```python
import jax
import jax.numpy as jnp
from jax import lax

HEADS = 16
NOPE = 128
ROPE = 64
VDIM = 128
RANK = 512
MOST = 5
NBLOCKS = 64
BLOCK = 512
TOKENS = 32768


def draw_queries(key, part):
    key = jax.random.fold_in(key, 11)
    first_key = jax.random.fold_in(key, 0)
    values = jnp.clip(jax.random.normal(first_key, (TOKENS, HEADS * (NOPE + ROPE)), jnp.float32), -6.0, 6.0)
    return values.astype(jnp.bfloat16)


def draw_block_mask(key, part):
    key = jax.random.fold_in(key, 7)
    count_key, score_key = jax.random.split(key)
    extra_counts = jax.random.randint(count_key, (NBLOCKS,), 0, MOST - 1)
    extra_counts = extra_counts.at[NBLOCKS - 1].set(MOST - 2)
    columns = jnp.arange(NBLOCKS, dtype=jnp.int32)[None, :]
    row_ids = jnp.arange(NBLOCKS, dtype=jnp.int32)[:, None]
    integer_scores = jax.random.randint(score_key, (NBLOCKS, NBLOCKS), 0, 1 << 20) * NBLOCKS + columns
    eligible = columns < row_ids - 1
    integer_scores = jnp.where(eligible, integer_scores, -1)
    ordering = jnp.argsort(-integer_scores, axis=1, stable=True)
    ranking = jnp.argsort(ordering, axis=1, stable=True)
    chosen = eligible & (ranking < extra_counts[:, None])
    result = chosen | (columns == row_ids) | (columns == row_ids - 1)
    return result.astype(jnp.int32)


def set_ends(entries, key, smallest, largest):
    longest = entries.shape.index(max(entries.shape))
    spots = []
    for shift in (0, 1):
        where = [jax.random.randint(jax.random.fold_in(key, axis), (), 0, length) for axis, length in enumerate(entries.shape)]
        where[longest] = (where[longest] + shift) % entries.shape[longest]
        spots.append(tuple(where))
    return entries.at[spots[0]].set(smallest).at[spots[1]].set(largest)


def shard_levels(stream_key, shape, pieces, smallest, largest):
    def one(axis_at, shards_of):
        draws = jax.random.uniform(jax.random.fold_in(jax.random.fold_in(stream_key, 6), axis_at), (shards_of,), jnp.float32, smallest / len(pieces), largest / len(pieces))
        return jnp.repeat(jnp.exp(draws), shape[axis_at] // shards_of).reshape((-1,) + (1,) * (len(shape) - axis_at - 1))

    level = one(*pieces[0])
    for cut in pieces[1:]:
        level = level * one(*cut)
    return level


def bell_draw(rng, shape, width, most, cuts=(), kind=jnp.bfloat16):
    factor_of = shard_levels(rng, shape, cuts, -0.22, 0.18) if cuts else 1.0
    values = jax.random.normal(rng, shape, jnp.float32) * width * factor_of
    return jnp.minimum(jnp.maximum(values, -most), most).astype(kind)


def setup_inputs(seed: int = 0) -> dict:
    splits = jax.random.split(jax.random.key(seed), 7)
    queries = draw_queries(jax.random.fold_in(splits[6], 71), 0)
    latent = bell_draw(splits[1], (TOKENS, RANK + ROPE), 1.0, 6.0, ((0, 256),))
    norm_gain = jnp.clip(1.0 + 0.1 * jax.random.normal(splits[2], (RANK,), jnp.float32), 0.5, 1.5)
    kv_up = bell_draw(splits[3], (RANK, HEADS * (NOPE + VDIM)), 128 ** -0.5, 0.5)
    block_mask = draw_block_mask(jax.random.fold_in(splits[6], 71), 0)
    positions = set_ends(jax.random.randint(splits[5], (TOKENS,), 0, TOKENS), jax.random.fold_in(splits[5], 1), 0, TOKENS - 1).astype(jnp.int32)
    return dict(queries=queries, latent=latent, norm_gain=norm_gain, kv_up=kv_up, block_mask=block_mask, positions=positions)


MASKED_SCORE = -1e+30
EPSILON = 1e-06

def rotate(values, angles):
    half = values.shape[-1] // 2
    first_half = values[..., :half]
    second_half = values[..., half:]
    cosine = jnp.cos(angles)
    sine = jnp.sin(angles)
    return jnp.concatenate([first_half * cosine - second_half * sine, second_half * cosine + first_half * sine], axis=-1)

def attend(carried, query_cat, key_block, allowed):
    weighted, running_max, running_sum = carried
    scores = jnp.einsum('rhc,kc->rhk', query_cat.astype(jnp.float32), key_block.astype(jnp.float32)) / jnp.sqrt(jnp.float32(NOPE + ROPE))
    scores = jnp.where(allowed[:, None, :], scores, MASKED_SCORE)
    new_max = jnp.maximum(running_max, scores.max(axis=-1))
    factor = jnp.exp(running_max - new_max)
    probs = jnp.where(allowed[:, None, :], jnp.exp(scores - new_max[..., None]), 0.0).astype(jnp.bfloat16)
    running_sum = running_sum * factor + probs.astype(jnp.float32).sum(axis=-1)
    weighted = weighted * factor[..., None] + jnp.einsum('rhk,kc->rhc', probs.astype(jnp.float32), key_block[:, :RANK].astype(jnp.float32))
    return (weighted, new_max, running_sum)

def reference(queries, latent, norm_gain, kv_up, block_mask, positions):
    inverse_freq = 10000.0 ** (-(jnp.arange(ROPE // 2, dtype=jnp.float32) * 2.0 / ROPE))
    angles = positions.astype(jnp.float32)[:, None] * inverse_freq[None, :]
    query_heads = queries.reshape(TOKENS, HEADS, NOPE + ROPE)
    up_heads = kv_up.reshape(RANK, HEADS, NOPE + VDIM)
    query_latent = jnp.einsum('thd,chd->thc', query_heads[..., :NOPE].astype(jnp.float32), up_heads[..., :NOPE].astype(jnp.float32)).astype(jnp.bfloat16)
    query_rope = rotate(query_heads[..., NOPE:].astype(jnp.float32), angles[:, None, :]).astype(jnp.bfloat16)
    query_cat = jnp.concatenate([query_latent, query_rope], axis=-1)
    compressed = latent[:, :RANK].astype(jnp.float32)
    key_latent = (compressed * lax.rsqrt(lax.optimization_barrier(jnp.mean(compressed * compressed, axis=-1, keepdims=True)) + EPSILON) * norm_gain).astype(jnp.bfloat16)
    key_rope = rotate(latent[:, RANK:].astype(jnp.float32), angles).astype(jnp.bfloat16)
    key_cat = jnp.concatenate([key_latent, key_rope], axis=-1)
    value_heads = up_heads[..., NOPE:].astype(jnp.float32)

    def one_block(block_index):
        first_row = block_index * BLOCK
        query_block = lax.dynamic_slice_in_dim(query_cat, first_row, BLOCK, 0)
        row_index = first_row + jnp.arange(BLOCK, dtype=jnp.int32)
        mask_row = block_mask[block_index]
        initial = (jnp.zeros((BLOCK, HEADS, RANK), jnp.float32), jnp.full((BLOCK, HEADS), MASKED_SCORE, jnp.float32), jnp.zeros((BLOCK, HEADS), jnp.float32))

        def visit(carried, source):
            key_block = lax.dynamic_slice_in_dim(key_cat, (source * BLOCK).astype(jnp.int32), BLOCK, 0)
            key_index = source * BLOCK + jnp.arange(BLOCK, dtype=jnp.int32)
            allowed = key_index[None, :] <= row_index[:, None]
            carried = lax.cond(mask_row[source] > 0, lambda kept: attend(kept, query_block, key_block, allowed), lambda kept: kept, carried)
            return (carried, None)
        (weighted, running_max, running_sum), _ = lax.scan(visit, initial, jnp.arange(NBLOCKS, dtype=jnp.int32))
        mixed = weighted / running_sum[..., None]
        output = jnp.einsum('thc,chv->thv', mixed, value_heads, precision=lax.Precision.HIGHEST)
        return output.astype(jnp.bfloat16).reshape(BLOCK, HEADS * VDIM)
    blocks_out = lax.map(one_block, jnp.arange(NBLOCKS, dtype=jnp.int32))
    return blocks_out.reshape(TOKENS, HEADS * VDIM)
```

```python
import math

import jax
import jax.numpy as jnp
import numpy as np
from jax import lax
from jax.experimental import pallas as pl
from jax.experimental.pallas import tpu as pltpu
from jax.sharding import PartitionSpec as P

HEADS = 16
NOPE = 128
ROPE = 64
VDIM = 128
RANK = 512
MOST = 5
EXTRA = MOST - 2
EPSILON = 1e-06
LOW = -1e30
SCALE = math.log2(math.e) / math.sqrt(NOPE + ROPE)
LANES = 128
ROWS = 128
BLOCK = 512
CAT = RANK + ROPE
WIDE = RANK + LANES
TOGETHER = 4
GROUPS = HEADS // TOGETHER
COLS = TOGETHER * ROWS
VT_ROWS = RANK + 16
Y, Z, CORES, X = 4, 8, 2, 4
HOME = 3
BLOCKS = Y * Z * CORES
PIECE = CAT // Y
HALF = Y // 2
SLOT = X * Y
F32 = jnp.float32
BF16 = jnp.bfloat16
NT = (((1,), (1,)), ((), ()))
NN = (((1,), (0,)), ((), ()))
MESH = pl.DeviceIdType.MESH

SPREAD = 0
INDEX = 1
BEFORE = 2
CORE = 3
SIDE = 4
ONWARD = 19
RING_UP = 24
RING_DOWN = 31
CHOSEN = 39
RECEIVES = 42
TO_Y, TO_INDEX, TO_RING, TO_X, TO_CHOSEN = range(5)
SENDS = 5
LOCALS = 7


def iota(shape, dim):
    return lax.broadcasted_iota(jnp.int32, shape, dim)


def frequencies():
    row = iota((ROPE // 2, LANES), 0)
    freq = jnp.zeros((ROPE // 2, LANES), F32)
    for i in range(ROPE // 2):
        freq = jnp.where(row == i, float(np.float32(10000.0 ** (-2.0 * i / ROPE))), freq)
    return freq


def turn(v, cosine, sine):
    u, w = v[: ROPE // 2], v[ROPE // 2 :]
    return jnp.concatenate([u * cosine - w * sine, w * cosine + u * sine], axis=0)


def kernel(
    q_hbm,
    latent_hbm,
    gain_hbm,
    up_hbm,
    mask_hbm,
    pos_hbm,
    out_ref,
    q_ref,
    latent_ref,
    gain_ref,
    up_ref,
    mask_ref,
    pos_ref,
    trig_ref,
    index_ref,
    index_smem,
    keys_ref,
    spread_ref,
    hold_ref,
    pick_ref,
    qt_ref,
    wvt_ref,
    k_ref,
    vt_ref,
    s_ref,
    o_ref,
    m_ref,
    send,
    recv,
    local,
):
    block = lax.axis_index("blk")
    x = lax.axis_index("kv")
    y = lax.div(block, Z * CORES)
    z = lax.rem(lax.div(block, CORES), Z)
    c = lax.rem(block, CORES)

    ups, downs = ((block, lax.rem(x + by, X)) for by in (1, X - 1))
    along_x = {1: ups, -1: downs}
    turned_y = [lax.rem(y + d, Y) for d in range(Y)]
    along_y = [(turned_y[d] * (Z * CORES) + z * CORES + c, x) for d in range(Y)]
    ups, downs = (
        (y * (Z * CORES) + lax.rem(z + by, Z) * CORES + c, x) for by in (1, Z - 1)
    )
    along_z = {1: ups, -1: downs}
    other_core = (block + 1 - 2 * c, x)
    after = (lax.rem(block + 1, BLOCKS), x)
    ahead = (lax.rem(block + BLOCKS - 1, BLOCKS), x)

    barrier = pltpu.get_barrier_semaphore()
    peers = [*along_x.values(), *along_y[1:], *along_z.values(), other_core, after, ahead]
    for peer in peers:
        pl.semaphore_signal(barrier, inc=1, device_id=peer, device_id_type=MESH)

    loads = [
        pltpu.make_async_copy(src, dst, local.at[i])
        for i, (src, dst) in enumerate(
            [
                (latent_hbm, latent_ref),
                (pos_hbm, pos_ref),
                (gain_hbm, gain_ref),
                (mask_hbm, mask_ref),
                (q_hbm, q_ref),
                (up_hbm, up_ref),
            ]
        )
    ]
    for load in loads:
        load.start()

    def pick_one(pieces, turn):
        one = pieces[0]
        for i in range(1, Y):
            one = jnp.where(turned_y[turn % Y] == i, pieces[i], one)
        return one

    def copy(src, dst, leaves, number, device):
        return pltpu.make_async_remote_copy(
            src_ref=src,
            dst_ref=dst,
            send_sem=send.at[leaves],
            recv_sem=recv.at[number],
            device_id=device,
            device_id_type=MESH,
        )

    def arrived(dst, number):
        copy(dst, dst, 0, number, other_core).wait_recv()

    loads[0].wait()
    loads[1].wait()
    loads[2].wait()
    angles = pos_ref[...].astype(F32) * frequencies()
    cosine = jnp.cos(angles)
    sine = jnp.sin(angles)
    trig_ref[0] = cosine
    trig_ref[1] = sine
    latent = latent_ref[:RANK, :].astype(F32)
    latent = latent * lax.rsqrt(jnp.mean(latent * latent, axis=0, keepdims=True) + EPSILON)
    gain = [
        jnp.broadcast_to(gain_ref[:, i * LANES : (i + 1) * LANES], (LANES, LANES)).T
        for i in range(RANK // LANES)
    ]
    rope = turn(latent_ref[RANK:, :].astype(F32), cosine, sine)
    cat = jnp.concatenate([latent * jnp.concatenate(gain, axis=0), rope], axis=0).astype(BF16)
    pieces = [cat[i * PIECE : (i + 1) * PIECE] for i in range(Y)]
    for i in range(Y):
        keys_ref[i] = pieces[i]
        spread_ref[i] = pick_one(pieces, i)
    hold_ref[HOME * Y] = pick_one(pieces, 0)

    pl.semaphore_wait(barrier, len(peers))

    def spread(d):
        return copy(spread_ref.at[d], hold_ref.at[HOME * Y + d], TO_Y, SPREAD, along_y[d])

    def tell(d):
        return copy(index_ref.at[0], index_ref.at[d], TO_INDEX, INDEX, along_y[d])

    def half(slot, quarter, i):
        return keys_ref.at[pl.ds(slot * SLOT + quarter * Y + i * HALF, HALF)]

    def side(slot):
        copies = []
        for i in range(2):
            up, down = half(slot, 0, i), half(slot, 0, 1 - i)
            number = SIDE + 3 * slot + 2 * i
            copies.append(copy(up, half(slot, 1, i), TO_X, number, along_x[1]))
            copies.append(
                copy(down, half(slot, 2, 1 - i), TO_X, number + 1 - i, along_x[-1])
            )
        return copies

    def onward(slot):
        return [
            copy(half(slot, 1, 0), half(slot, 3, 0), TO_X, ONWARD + slot, along_x[1]),
            copy(half(slot, 2, 1), half(slot, 3, 1), TO_X, ONWARD + slot, along_x[-1]),
        ]

    def start(copies):
        for each in copies:
            each.start()

    def side_event(slot):
        arrived(half(slot, 1, 0), SIDE + 3 * slot)
        arrived(half(slot, 2, 1), SIDE + 3 * slot + 1)
        start(onward(slot))

    def sides_arrived(slot):
        arrived(keys_ref.at[pl.ds(slot * SLOT + Y + HALF, Y)], SIDE + 3 * slot + 2)

    def onward_arrived(slot):
        arrived(keys_ref.at[pl.ds(slot * SLOT + 3 * Y, Y)], ONWARD + slot)

    for d in range(1, Y):
        spread(d).start()
    own = keys_ref.at[pl.ds(0, Y)]
    before = copy(own, keys_ref.at[pl.ds(SLOT, Y)], TO_RING, BEFORE, after)
    before.start()
    start(side(0))

    def chunk(steps, core, first=0, size=Y):
        base = (core * Z + (steps + HOME) % Z) * Y
        return hold_ref.at[pl.ds(base + first, size)]

    def up_part(k):
        return (0, 1) if k == 6 else (HALF * (k % 2), HALF)

    def down_part(k):
        return (1, 1) if k == 7 else (HALF * (1 - k % 2), HALF)

    def ring(k):
        step = k // 2
        copies = []
        if k < 7:
            part = up_part(k)
            src, dst = chunk(step, 0, *part), chunk(step + 1, 0, *part)
            copies.append(copy(src, dst, TO_RING, RING_UP + k, along_z[1]))
        part = down_part(k)
        src, dst = chunk(-step, 0, *part), chunk(-step - 1, 0, *part)
        copies.append(copy(src, dst, TO_RING, RING_DOWN + k, along_z[-1]))
        return copies

    def to_core(first, chunks):
        src = hold_ref.at[pl.ds(first * Y, chunks * Y)]
        dst = hold_ref.at[pl.ds((Z + first) * Y, chunks * Y)]
        copy(src, dst, TO_RING, CORE, other_core).start()

    def ring_event(k):
        step = k // 2
        if k < 7:
            arrived(chunk(step + 1, 0, *up_part(k)), RING_UP + k)
        arrived(chunk(-step - 1, 0, *down_part(k)), RING_DOWN + k)
        if k < 6:
            start(ring(k + 2))
        if k == 3:
            to_core(1, 5)
        if k == 5:
            to_core(0, 1)
            to_core(6, 1)
        if k == 7:
            to_core(7, 1)

    def core_arrived():
        arrived(hold_ref.at[pl.ds(Z * Y, Z * Y)], CORE)

    loads[4].wait()
    loads[5].wait()

    def absorb(group, _):
        cosine, sine = trig_ref[0], trig_ref[1]
        none = jnp.zeros((ROWS, NOPE), BF16)
        low = iota((ROWS, LANES), 1) < ROPE
        for i in range(TOGETHER // 2):
            pair = group * (TOGETHER // 2) + i
            cols = slice(2 * i * ROWS, 2 * (i + 1) * ROWS)
            q = q_ref[:, pl.ds(pl.multiple_of(pair * 384, 384), 384)]
            up = up_ref[:, pl.ds(pl.multiple_of(pair * 512, 512), 512)]
            q1 = q[:, LANES : 2 * LANES].astype(F32)
            q2 = q[:, 2 * LANES :].astype(F32)
            nope_b = jnp.where(low, pltpu.roll(q1, ROPE, 1), pltpu.roll(q2, ROPE, 1))
            pe = jnp.where(low, q1, q2).T
            nope = jnp.concatenate(
                [
                    jnp.concatenate([q[:, :LANES], none], axis=1),
                    jnp.concatenate([none, nope_b.astype(BF16)], axis=1),
                ],
                axis=0,
            )
            w_key = jnp.concatenate([up[:, :NOPE], up[:, 2 * NOPE : 3 * NOPE]], axis=1)
            lat = lax.dot_general(w_key, nope, NT, preferred_element_type=F32)
            qt_ref[group, :RANK, cols] = lat.astype(BF16)
            rope = [turn(pe[:ROPE], cosine, sine), turn(pe[ROPE:], cosine, sine)]
            qt_ref[group, RANK:CAT, cols] = jnp.concatenate(rope, axis=1).astype(BF16)
            qt_ref[group, CAT:, cols] = jnp.zeros((WIDE - CAT, 2 * ROWS), BF16)
            for head in range(2):
                w_value = up[:, (2 * head + 1) * NOPE : (2 * head + 2) * NOPE]
                wvt_ref[group, 2 * i + head] = w_value.T
        return 0

    absorb(0, 0)
    arrived(hold_ref.at[pl.ds(HOME * Y + 1, Y - 1)], SPREAD)
    start(ring(0))
    start(ring(1))
    side_event(0)
    arrived(keys_ref.at[pl.ds(SLOT, Y)], BEFORE)
    start(side(1))

    def find(j, found):
        count, first, second, third = found
        hit = jnp.where(j < block - 1, mask_ref[0, j], 0) > 0
        first = jnp.where(hit & (count == 0), j, first)
        second = jnp.where(hit & (count == 1), j, second)
        third = jnp.where(hit & (count == 2), j, third)
        return (jnp.where(hit, count + 1, count), first, second, third)

    loads[3].wait()
    zero = jnp.int32(0)
    count, *chosen = lax.fori_loop(0, BLOCKS, find, (zero,) * 4, unroll=8)
    column = iota((8, LANES), 1)
    index = jnp.zeros((8, LANES), jnp.int32)
    for e, j in enumerate(chosen):
        far_core = (j + c) & (CORES - 1)
        far_z = (z - (j >> 1) + HOME + Z) & (Z - 1)
        index = jnp.where(column == e, (far_core * Z + far_z) * Y + (j >> 4), index)
    index_ref[0] = index
    for d in range(1, Y):
        tell(d).start()

    vt_ref[RANK:, :] = jnp.ones((VT_ROWS - RANK, BLOCK), BF16)

    def unpack(*quarters):
        for place, (slot, quarter) in enumerate(quarters):
            cols = slice(place * ROWS, (place + 1) * ROWS)
            cat = [keys_ref[slot * SLOT + quarter * Y + i] for i in range(Y)]
            if not (isinstance(slot, int) and slot < 2):
                cat = [pick_one(cat, -i) for i in range(Y)]
            cat = jnp.concatenate(cat + [jnp.zeros((WIDE - CAT, ROWS), BF16)], axis=0)
            vt_ref[:RANK, cols] = cat[:RANK]
            for i in range(WIDE // LANES):
                rows = slice(i * LANES, (i + 1) * LANES)
                k_ref[cols, rows] = cat[rows].T

    def finish(group, o):
        total = o[RANK : RANK + 1, :]
        high = o[:RANK].astype(BF16)
        rest = (o[:RANK] - high.astype(F32)).astype(BF16)
        outs = []
        for head in range(TOGETHER):
            cols = slice(head * ROWS, (head + 1) * ROWS)
            both = jnp.concatenate([high[:, cols], rest[:, cols]], axis=1)
            got = lax.dot_general(wvt_ref[group, head], both, NN, preferred_element_type=F32)
            outs.append(((got[:, :ROWS] + got[:, ROWS:]) / total[:, cols]).T)
        out_ref[:, pl.ds(pl.multiple_of(group * COLS, COLS), COLS)] = jnp.concatenate(
            outs, axis=1
        ).astype(BF16)

    def attend(first, units, groups, diagonal=False, last=False):
        total = sum(size for size, _ in groups)
        starts = [sum(size for size, _ in groups[:i]) for i in range(len(groups))]
        groups = [(slice(at, at + size), valid) for at, (size, valid) in zip(starts, groups)]

        def score(unit):
            group = first + unit
            s = lax.dot_general(k_ref[:total, :], qt_ref[group], NN, preferred_element_type=F32)
            if diagonal:
                key = iota((ROWS, COLS), 0)
                token = iota((ROWS, COLS), 1) & (ROWS - 1)
                parts = [jnp.where(key <= token, s[:ROWS], LOW)]
                for quarter, steps in ((1, 1), (2, 3), (3, 2)):
                    rows = slice(quarter * ROWS, (quarter + 1) * ROWS)
                    parts.append(jnp.where(steps <= x, s[rows], LOW))
                s = jnp.concatenate(parts, axis=0)
            s_ref[unit % 2, :total, :] = s
            return [jnp.max(s[keys], axis=0, keepdims=True) for keys, _ in groups]

        def weigh(unit, tops):
            group = first + unit
            if diagonal:
                m = tops[0]
            else:
                m_old = m_ref[group, :1, :]
                m = m_old
                for top, (_, valid) in zip(tops, groups):
                    m = jnp.maximum(m, jnp.where(valid, top, LOW))
            p = []
            for keys, valid in groups:
                m_used = m if diagonal else jnp.where(valid, m, -LOW)
                p.append(jnp.exp2((s_ref[unit % 2, keys, :] - m_used) * SCALE).astype(BF16))
            p = p[0] if len(p) == 1 else jnp.concatenate(p, axis=0)
            o = lax.dot_general(vt_ref[:, :total], p, NN, preferred_element_type=F32)
            if not diagonal:
                o = o_ref[group] * jnp.exp2((m_old - m) * SCALE) + o
                if last:
                    finish(group, o)
                    return
            o_ref[group] = o
            m_ref[group] = jnp.broadcast_to(m, (8, COLS))

        tops = {unit: score(unit) for unit in range(min(2, units))}
        for unit in range(units):
            weigh(unit, tops[unit])
            if unit + 2 < units:
                tops[unit + 2] = score(unit + 2)

    for k in range(3):
        ring_event(k)
        absorb(1 + k, 0)
    side_event(1)
    sides_arrived(0)
    onward_arrived(0)
    unpack(*((0, quarter) for quarter in range(X)))
    ring_event(3)
    for i in range(3):
        attend(i, 1, [(BLOCK, True)], diagonal=True)
        ring_event(4 + i)
    ring_event(7)

    arrived(index_ref.at[pl.ds(1, Y - 1)], INDEX)
    to_smem = pltpu.make_async_copy(index_ref, index_smem, local.at[6])
    to_smem.start()
    core_arrived()
    to_smem.wait()

    def chosen_copy(e, d):
        src = pick_ref.at[3 * e + d - 1]
        return copy(src, keys_ref.at[(2 + e) * SLOT + d], TO_CHOSEN, CHOSEN + e, along_y[d])

    def place(e, d):
        told = index_smem[(Y - d) % Y, 0, e]
        return (told & -Y) + ((y - told) & (Y - 1))

    for e in range(EXTRA):
        for d in range(1, Y):
            pick_ref[3 * e + d - 1] = hold_ref[place(e, d)]
            chosen_copy(e, d).start()
        keys_ref[(2 + e) * SLOT] = hold_ref[place(e, 0)]

    def chosen_arrived(e):
        arrived(keys_ref.at[pl.ds((2 + e) * SLOT + 1, Y - 1)], CHOSEN + e)

    attend(3, 1, [(BLOCK, True)], diagonal=True)
    sides_arrived(1)
    onward_arrived(1)
    unpack(*((1, quarter) for quarter in range(X)))
    for e in range(EXTRA):
        chosen_arrived(e)
        start(side(2 + e))

    attend(0, GROUPS, [(BLOCK, block > 0)])
    side_event(2)

    def chosen_block(e, _):
        sides_arrived(2 + e)
        unpack(*((2 + e, quarter) for quarter in range(3)))
        attend(0, GROUPS, [(3 * ROWS, count > e)])
        pl.when(e < EXTRA - 1)(lambda: side_event(3 + e))
        return 0

    lax.fori_loop(0, EXTRA, chosen_block, 0)
    for e in range(EXTRA):
        onward_arrived(2 + e)
    unpack(*((2 + e, 3) for e in range(EXTRA)))
    attend(0, GROUPS, [(ROWS, count > e) for e in range(EXTRA)], last=True)

    for leaves, whole in (
        (TO_Y, spread_ref.at[pl.ds(1, Y - 1)]),
        (TO_INDEX, index_ref.at[pl.ds(1, Y - 1)]),
        (TO_RING, hold_ref),
        (TO_X, keys_ref.at[pl.ds(0, 3 * MOST * Y)]),
        (TO_CHOSEN, pick_ref),
    ):
        copy(whole, whole, leaves, 0, other_core).wait_send()


def per_device(queries, latent, norm_gain, kv_up, block_mask, positions):
    anywhere = pl.BlockSpec(memory_space=pl.ANY)
    return pl.pallas_call(
        kernel,
        out_shape=jax.ShapeDtypeStruct((ROWS, HEADS * VDIM), BF16),
        in_specs=[anywhere] * 6,
        out_specs=pl.BlockSpec(memory_space=pltpu.VMEM),
        scratch_shapes=[
            pltpu.VMEM((ROWS, HEADS * (NOPE + ROPE)), BF16),
            pltpu.VMEM((CAT, ROWS), BF16),
            pltpu.VMEM((1, RANK), F32),
            pltpu.VMEM((RANK, HEADS * (NOPE + VDIM)), BF16),
            pltpu.SMEM((1, BLOCKS), jnp.int32),
            pltpu.VMEM((1, ROWS), jnp.int32),
            pltpu.VMEM((2, ROPE // 2, LANES), F32),
            pltpu.VMEM((Y, 8, LANES), jnp.int32),
            pltpu.SMEM((Y, 8, LANES), jnp.int32),
            pltpu.VMEM((MOST * SLOT, PIECE, ROWS), BF16),
            pltpu.VMEM((Y, PIECE, ROWS), BF16),
            pltpu.VMEM((BLOCKS, PIECE, ROWS), BF16),
            pltpu.VMEM((EXTRA * (Y - 1), PIECE, ROWS), BF16),
            pltpu.VMEM((GROUPS, WIDE, COLS), BF16),
            pltpu.VMEM((GROUPS, TOGETHER, VDIM, RANK), BF16),
            pltpu.VMEM((BLOCK, WIDE), BF16),
            pltpu.VMEM((VT_ROWS, BLOCK), BF16),
            pltpu.VMEM((2, BLOCK, COLS), F32),
            pltpu.VMEM((GROUPS, VT_ROWS, COLS), F32),
            pltpu.VMEM((GROUPS, 8, COLS), F32),
            pltpu.SemaphoreType.DMA((SENDS,)),
            pltpu.SemaphoreType.DMA((RECEIVES,)),
            pltpu.SemaphoreType.DMA((LOCALS,)),
        ],
        compiler_params=pltpu.CompilerParams(
            collective_id=0, has_side_effects=True, vmem_limit_bytes=56 * 1024 * 1024
        ),
        cost_estimate=pl.CostEstimate(
            flops=13_000_000_000, bytes_accessed=6_000_000, transcendentals=5_000_000
        ),
    )(
        queries,
        latent.T,
        norm_gain.reshape(1, RANK),
        kv_up,
        block_mask,
        positions.reshape(1, ROWS),
    )


def solution(mesh):
    in_specs = (
        P(("blk", "kv"), None),
        P(("blk", "kv"), None),
        P(),
        P(),
        P("blk", None),
        P(("blk", "kv")),
    )
    return jax.shard_map(
        per_device, mesh=mesh, in_specs=in_specs, out_specs=P(("blk", "kv"), None), check_vma=False
    )
```

```python
import math

import jax
import jax.numpy as jnp
import numpy as np
from jax import lax
from jax.experimental import pallas as pl
from jax.experimental.pallas import tpu as pltpu
from jax.sharding import PartitionSpec as P

HEADS = 16
NOPE = 128
ROPE = 64
VDIM = 128
RANK = 512
MOST = 5
EXTRA = MOST - 2
EPSILON = 1e-06
LOW = -1e30
SCALE = math.log2(math.e) / math.sqrt(NOPE + ROPE)
LANES = 128
ROWS = 128
BLOCK = 512
CAT = RANK + ROPE
WIDE = RANK + LANES
TOGETHER = 8
GROUPS = HEADS // TOGETHER
COLS = TOGETHER * ROWS
VT_ROWS = RANK + 16
Y, Z, CORES, X = 4, 8, 2, 4
HOME = 3
BLOCKS = Y * Z * CORES
PIECE = CAT // Y
HALF = Y // 2
SLOT = X * Y
F32 = jnp.float32
BF16 = jnp.bfloat16
NT = (((1,), (1,)), ((), ()))
NN = (((1,), (0,)), ((), ()))
MESH = pl.DeviceIdType.MESH

SPREAD = 0
INDEX = 1
BEFORE = 2
CORE = 3
SIDE = 4
ONWARD = 19
RING_UP = 24
RING_DOWN = 31
CHOSEN = 39
RECEIVES = 42
TO_Y, TO_INDEX, TO_RING, TO_X, TO_CHOSEN = range(5)
SENDS = 5
LOCALS = 7


def iota(shape, dim):
    return lax.broadcasted_iota(jnp.int32, shape, dim)


def frequencies():
    row = iota((ROPE // 2, LANES), 0)
    freq = jnp.zeros((ROPE // 2, LANES), F32)
    for i in range(ROPE // 2):
        freq = jnp.where(row == i, float(np.float32(10000.0 ** (-2.0 * i / ROPE))), freq)
    return freq


def turn(v, cosine, sine):
    u, w = v[: ROPE // 2], v[ROPE // 2 :]
    return jnp.concatenate([u * cosine - w * sine, w * cosine + u * sine], axis=0)


def kernel(
    q_hbm,
    latent_hbm,
    gain_hbm,
    up_hbm,
    mask_hbm,
    pos_hbm,
    out_ref,
    q_ref,
    latent_ref,
    gain_ref,
    up_ref,
    mask_ref,
    pos_ref,
    trig_ref,
    index_ref,
    index_smem,
    keys_ref,
    spread_ref,
    hold_ref,
    pick_ref,
    qt_ref,
    wvt_ref,
    k_ref,
    vt_ref,
    s_ref,
    o_ref,
    m_ref,
    send,
    recv,
    local,
):
    block = lax.axis_index("blk")
    x = lax.axis_index("kv")
    y = lax.div(block, Z * CORES)
    z = lax.rem(lax.div(block, CORES), Z)
    c = lax.rem(block, CORES)

    ups, downs = ((block, lax.rem(x + by, X)) for by in (1, X - 1))
    along_x = {1: ups, -1: downs}
    turned_y = [lax.rem(y + d, Y) for d in range(Y)]
    along_y = [(turned_y[d] * (Z * CORES) + z * CORES + c, x) for d in range(Y)]
    ups, downs = (
        (y * (Z * CORES) + lax.rem(z + by, Z) * CORES + c, x) for by in (1, Z - 1)
    )
    along_z = {1: ups, -1: downs}
    other_core = (block + 1 - 2 * c, x)
    after = (lax.rem(block + 1, BLOCKS), x)
    ahead = (lax.rem(block + BLOCKS - 1, BLOCKS), x)

    barrier = pltpu.get_barrier_semaphore()
    peers = [*along_x.values(), *along_y[1:], *along_z.values(), other_core, after, ahead]
    for peer in peers:
        pl.semaphore_signal(barrier, inc=1, device_id=peer, device_id_type=MESH)

    loads = [
        pltpu.make_async_copy(src, dst, local.at[i])
        for i, (src, dst) in enumerate(
            [
                (latent_hbm, latent_ref),
                (pos_hbm, pos_ref),
                (gain_hbm, gain_ref),
                (mask_hbm, mask_ref),
                (q_hbm, q_ref),
                (up_hbm, up_ref),
            ]
        )
    ]
    for load in loads:
        load.start()

    def pick_one(pieces, turn):
        one = pieces[0]
        for i in range(1, Y):
            one = jnp.where(turned_y[turn % Y] == i, pieces[i], one)
        return one

    def copy(src, dst, leaves, number, device):
        return pltpu.make_async_remote_copy(
            src_ref=src,
            dst_ref=dst,
            send_sem=send.at[leaves],
            recv_sem=recv.at[number],
            device_id=device,
            device_id_type=MESH,
        )

    def arrived(dst, number):
        copy(dst, dst, 0, number, other_core).wait_recv()

    loads[0].wait()
    loads[1].wait()
    loads[2].wait()
    angles = pos_ref[...].astype(F32) * frequencies()
    cosine = jnp.cos(angles)
    sine = jnp.sin(angles)
    trig_ref[0] = cosine
    trig_ref[1] = sine
    latent = latent_ref[:RANK, :].astype(F32)
    latent = latent * lax.rsqrt(jnp.mean(latent * latent, axis=0, keepdims=True) + EPSILON)
    gain = [
        jnp.broadcast_to(gain_ref[:, i * LANES : (i + 1) * LANES], (LANES, LANES)).T
        for i in range(RANK // LANES)
    ]
    rope = turn(latent_ref[RANK:, :].astype(F32), cosine, sine)
    cat = jnp.concatenate([latent * jnp.concatenate(gain, axis=0), rope], axis=0).astype(BF16)
    pieces = [cat[i * PIECE : (i + 1) * PIECE] for i in range(Y)]
    for i in range(Y):
        keys_ref[i] = pieces[i]
        spread_ref[i] = pick_one(pieces, i)
    hold_ref[HOME * Y] = pick_one(pieces, 0)

    pl.semaphore_wait(barrier, len(peers))

    def spread(d):
        return copy(spread_ref.at[d], hold_ref.at[HOME * Y + d], TO_Y, SPREAD, along_y[d])

    def tell(d):
        return copy(index_ref.at[0], index_ref.at[d], TO_INDEX, INDEX, along_y[d])

    def half(slot, quarter, i):
        return keys_ref.at[pl.ds(slot * SLOT + quarter * Y + i * HALF, HALF)]

    def side(slot):
        copies = []
        for i in range(2):
            up, down = half(slot, 0, i), half(slot, 0, 1 - i)
            number = SIDE + 3 * slot + 2 * i
            copies.append(copy(up, half(slot, 1, i), TO_X, number, along_x[1]))
            copies.append(
                copy(down, half(slot, 2, 1 - i), TO_X, number + 1 - i, along_x[-1])
            )
        return copies

    def onward(slot):
        return [
            copy(half(slot, 1, 0), half(slot, 3, 0), TO_X, ONWARD + slot, along_x[1]),
            copy(half(slot, 2, 1), half(slot, 3, 1), TO_X, ONWARD + slot, along_x[-1]),
        ]

    def start(copies):
        for each in copies:
            each.start()

    def side_event(slot):
        arrived(half(slot, 1, 0), SIDE + 3 * slot)
        arrived(half(slot, 2, 1), SIDE + 3 * slot + 1)
        start(onward(slot))

    def sides_arrived(slot):
        arrived(keys_ref.at[pl.ds(slot * SLOT + Y + HALF, Y)], SIDE + 3 * slot + 2)

    def onward_arrived(slot):
        arrived(keys_ref.at[pl.ds(slot * SLOT + 3 * Y, Y)], ONWARD + slot)

    for d in range(1, Y):
        spread(d).start()
    own = keys_ref.at[pl.ds(0, Y)]
    before = copy(own, keys_ref.at[pl.ds(SLOT, Y)], TO_RING, BEFORE, after)
    before.start()
    start(side(0))

    def chunk(steps, core, first=0, size=Y):
        base = (core * Z + (steps + HOME) % Z) * Y
        return hold_ref.at[pl.ds(base + first, size)]

    def up_part(k):
        return (0, 1) if k == 6 else (HALF * (k % 2), HALF)

    def down_part(k):
        return (1, 1) if k == 7 else (HALF * (1 - k % 2), HALF)

    def ring(k):
        step = k // 2
        copies = []
        if k < 7:
            part = up_part(k)
            src, dst = chunk(step, 0, *part), chunk(step + 1, 0, *part)
            copies.append(copy(src, dst, TO_RING, RING_UP + k, along_z[1]))
        part = down_part(k)
        src, dst = chunk(-step, 0, *part), chunk(-step - 1, 0, *part)
        copies.append(copy(src, dst, TO_RING, RING_DOWN + k, along_z[-1]))
        return copies

    def to_core(first, chunks):
        src = hold_ref.at[pl.ds(first * Y, chunks * Y)]
        dst = hold_ref.at[pl.ds((Z + first) * Y, chunks * Y)]
        copy(src, dst, TO_RING, CORE, other_core).start()

    def ring_event(k):
        step = k // 2
        if k < 7:
            arrived(chunk(step + 1, 0, *up_part(k)), RING_UP + k)
        arrived(chunk(-step - 1, 0, *down_part(k)), RING_DOWN + k)
        if k < 6:
            start(ring(k + 2))
        if k == 3:
            to_core(1, 5)
        if k == 5:
            to_core(0, 1)
            to_core(6, 1)
        if k == 7:
            to_core(7, 1)

    def core_arrived():
        arrived(hold_ref.at[pl.ds(Z * Y, Z * Y)], CORE)

    loads[4].wait()
    loads[5].wait()

    def absorb(group, _):
        cosine, sine = trig_ref[0], trig_ref[1]
        none = jnp.zeros((ROWS, NOPE), BF16)
        low = iota((ROWS, LANES), 1) < ROPE
        for i in range(TOGETHER // 2):
            pair = group * (TOGETHER // 2) + i
            cols = slice(2 * i * ROWS, 2 * (i + 1) * ROWS)
            q = q_ref[:, pl.ds(pl.multiple_of(pair * 384, 384), 384)]
            up = up_ref[:, pl.ds(pl.multiple_of(pair * 512, 512), 512)]
            q1 = q[:, LANES : 2 * LANES].astype(F32)
            q2 = q[:, 2 * LANES :].astype(F32)
            nope_b = jnp.where(low, pltpu.roll(q1, ROPE, 1), pltpu.roll(q2, ROPE, 1))
            pe = jnp.where(low, q1, q2).T
            nope = jnp.concatenate(
                [
                    jnp.concatenate([q[:, :LANES], none], axis=1),
                    jnp.concatenate([none, nope_b.astype(BF16)], axis=1),
                ],
                axis=0,
            )
            w_key = jnp.concatenate([up[:, :NOPE], up[:, 2 * NOPE : 3 * NOPE]], axis=1)
            lat = lax.dot_general(w_key, nope, NT, preferred_element_type=F32)
            qt_ref[group, :RANK, cols] = lat.astype(BF16)
            rope = [turn(pe[:ROPE], cosine, sine), turn(pe[ROPE:], cosine, sine)]
            qt_ref[group, RANK:CAT, cols] = jnp.concatenate(rope, axis=1).astype(BF16)
            qt_ref[group, CAT:, cols] = jnp.zeros((WIDE - CAT, 2 * ROWS), BF16)
            for head in range(2):
                w_value = up[:, (2 * head + 1) * NOPE : (2 * head + 2) * NOPE]
                wvt_ref[group, 2 * i + head] = w_value.T
        return 0

    arrived(hold_ref.at[pl.ds(HOME * Y + 1, Y - 1)], SPREAD)
    start(ring(0))
    start(ring(1))
    side_event(0)
    arrived(keys_ref.at[pl.ds(SLOT, Y)], BEFORE)
    start(side(1))

    def find(j, found):
        count, first, second, third = found
        hit = jnp.where(j < block - 1, mask_ref[0, j], 0) > 0
        first = jnp.where(hit & (count == 0), j, first)
        second = jnp.where(hit & (count == 1), j, second)
        third = jnp.where(hit & (count == 2), j, third)
        return (jnp.where(hit, count + 1, count), first, second, third)

    loads[3].wait()
    zero = jnp.int32(0)
    count, *chosen = lax.fori_loop(0, BLOCKS, find, (zero,) * 4, unroll=8)
    column = iota((8, LANES), 1)
    index = jnp.zeros((8, LANES), jnp.int32)
    for e, j in enumerate(chosen):
        far_core = (j + c) & (CORES - 1)
        far_z = (z - (j >> 1) + HOME + Z) & (Z - 1)
        index = jnp.where(column == e, (far_core * Z + far_z) * Y + (j >> 4), index)
    index_ref[0] = index
    for d in range(1, Y):
        tell(d).start()
    lax.fori_loop(0, GROUPS, absorb, 0)

    vt_ref[RANK:, :] = jnp.ones((VT_ROWS - RANK, BLOCK), BF16)

    def unpack(*quarters):
        for place, (slot, quarter) in enumerate(quarters):
            cols = slice(place * ROWS, (place + 1) * ROWS)
            cat = [keys_ref[slot * SLOT + quarter * Y + i] for i in range(Y)]
            if not (isinstance(slot, int) and slot < 2):
                cat = [pick_one(cat, -i) for i in range(Y)]
            cat = jnp.concatenate(cat + [jnp.zeros((WIDE - CAT, ROWS), BF16)], axis=0)
            vt_ref[:RANK, cols] = cat[:RANK]
            for i in range(WIDE // LANES):
                rows = slice(i * LANES, (i + 1) * LANES)
                k_ref[cols, rows] = cat[rows].T

    def finish(group, o):
        total = o[RANK : RANK + 1, :]
        high = o[:RANK].astype(BF16)
        rest = (o[:RANK] - high.astype(F32)).astype(BF16)
        outs = []
        for head in range(TOGETHER):
            cols = slice(head * ROWS, (head + 1) * ROWS)
            both = jnp.concatenate([high[:, cols], rest[:, cols]], axis=1)
            got = lax.dot_general(wvt_ref[group, head], both, NN, preferred_element_type=F32)
            outs.append(((got[:, :ROWS] + got[:, ROWS:]) / total[:, cols]).T)
        out_ref[:, pl.ds(pl.multiple_of(group * COLS, COLS), COLS)] = jnp.concatenate(
            outs, axis=1
        ).astype(BF16)

    def attend(first, units, groups, diagonal=False, last=False):
        total = sum(size for size, _ in groups)
        starts = [sum(size for size, _ in groups[:i]) for i in range(len(groups))]
        groups = [(slice(at, at + size), valid) for at, (size, valid) in zip(starts, groups)]

        def score(unit):
            group = first + unit
            s = lax.dot_general(k_ref[:total, :], qt_ref[group], NN, preferred_element_type=F32)
            if diagonal:
                key = iota((ROWS, COLS), 0)
                token = iota((ROWS, COLS), 1) & (ROWS - 1)
                parts = [jnp.where(key <= token, s[:ROWS], LOW)]
                for quarter, steps in ((1, 1), (2, 3), (3, 2)):
                    rows = slice(quarter * ROWS, (quarter + 1) * ROWS)
                    parts.append(jnp.where(steps <= x, s[rows], LOW))
                s = jnp.concatenate(parts, axis=0)
            s_ref[unit % 2, :total, :] = s
            return [jnp.max(s[keys], axis=0, keepdims=True) for keys, _ in groups]

        def weigh(unit, tops):
            group = first + unit
            if diagonal:
                m = tops[0]
            else:
                m_old = m_ref[group, :1, :]
                m = m_old
                for top, (_, valid) in zip(tops, groups):
                    m = jnp.maximum(m, jnp.where(valid, top, LOW))
            p = []
            for keys, valid in groups:
                m_used = m if diagonal else jnp.where(valid, m, -LOW)
                p.append(jnp.exp2((s_ref[unit % 2, keys, :] - m_used) * SCALE).astype(BF16))
            p = p[0] if len(p) == 1 else jnp.concatenate(p, axis=0)
            o = lax.dot_general(vt_ref[:, :total], p, NN, preferred_element_type=F32)
            if not diagonal:
                o = o_ref[group] * jnp.exp2((m_old - m) * SCALE) + o
                if last:
                    finish(group, o)
                    return
            o_ref[group] = o
            m_ref[group] = jnp.broadcast_to(m, (8, COLS))

        tops = {unit: score(unit) for unit in range(min(2, units))}
        for unit in range(units):
            weigh(unit, tops[unit])
            if unit + 2 < units:
                tops[unit + 2] = score(unit + 2)

    ring_event(0)
    ring_event(1)
    ring_event(2)
    side_event(1)
    sides_arrived(0)
    onward_arrived(0)
    unpack(*((0, quarter) for quarter in range(X)))
    ring_event(3)
    attend(0, 1, [(BLOCK, True)], diagonal=True)
    for k in range(4, 8):
        ring_event(k)

    arrived(index_ref.at[pl.ds(1, Y - 1)], INDEX)
    to_smem = pltpu.make_async_copy(index_ref, index_smem, local.at[6])
    to_smem.start()
    core_arrived()
    to_smem.wait()

    def chosen_copy(e, d):
        src = pick_ref.at[3 * e + d - 1]
        return copy(src, keys_ref.at[(2 + e) * SLOT + d], TO_CHOSEN, CHOSEN + e, along_y[d])

    def place(e, d):
        told = index_smem[(Y - d) % Y, 0, e]
        return (told & -Y) + ((y - told) & (Y - 1))

    for e in range(EXTRA):
        for d in range(1, Y):
            pick_ref[3 * e + d - 1] = hold_ref[place(e, d)]
            chosen_copy(e, d).start()
        keys_ref[(2 + e) * SLOT] = hold_ref[place(e, 0)]

    def chosen_arrived(e):
        arrived(keys_ref.at[pl.ds((2 + e) * SLOT + 1, Y - 1)], CHOSEN + e)

    attend(1, 1, [(BLOCK, True)], diagonal=True)
    sides_arrived(1)
    onward_arrived(1)
    unpack(*((1, quarter) for quarter in range(X)))
    for e in range(EXTRA):
        chosen_arrived(e)
        start(side(2 + e))

    attend(0, GROUPS, [(BLOCK, block > 0)])
    side_event(2)

    def chosen_block(e, _):
        sides_arrived(2 + e)
        unpack(*((2 + e, quarter) for quarter in range(3)))
        attend(0, GROUPS, [(3 * ROWS, count > e)])
        pl.when(e < EXTRA - 1)(lambda: side_event(3 + e))
        return 0

    lax.fori_loop(0, EXTRA, chosen_block, 0)
    for e in range(EXTRA):
        onward_arrived(2 + e)
    unpack(*((2 + e, 3) for e in range(EXTRA)))
    attend(0, GROUPS, [(ROWS, count > e) for e in range(EXTRA)], last=True)

    for leaves, whole in (
        (TO_Y, spread_ref.at[pl.ds(1, Y - 1)]),
        (TO_INDEX, index_ref.at[pl.ds(1, Y - 1)]),
        (TO_RING, hold_ref),
        (TO_X, keys_ref.at[pl.ds(0, 3 * MOST * Y)]),
        (TO_CHOSEN, pick_ref),
    ):
        copy(whole, whole, leaves, 0, other_core).wait_send()


def per_device(queries, latent, norm_gain, kv_up, block_mask, positions):
    anywhere = pl.BlockSpec(memory_space=pl.ANY)
    return pl.pallas_call(
        kernel,
        out_shape=jax.ShapeDtypeStruct((ROWS, HEADS * VDIM), BF16),
        in_specs=[anywhere] * 6,
        out_specs=pl.BlockSpec(memory_space=pltpu.VMEM),
        scratch_shapes=[
            pltpu.VMEM((ROWS, HEADS * (NOPE + ROPE)), BF16),
            pltpu.VMEM((CAT, ROWS), BF16),
            pltpu.VMEM((1, RANK), F32),
            pltpu.VMEM((RANK, HEADS * (NOPE + VDIM)), BF16),
            pltpu.SMEM((1, BLOCKS), jnp.int32),
            pltpu.VMEM((1, ROWS), jnp.int32),
            pltpu.VMEM((2, ROPE // 2, LANES), F32),
            pltpu.VMEM((Y, 8, LANES), jnp.int32),
            pltpu.SMEM((Y, 8, LANES), jnp.int32),
            pltpu.VMEM((MOST * SLOT, PIECE, ROWS), BF16),
            pltpu.VMEM((Y, PIECE, ROWS), BF16),
            pltpu.VMEM((BLOCKS, PIECE, ROWS), BF16),
            pltpu.VMEM((EXTRA * (Y - 1), PIECE, ROWS), BF16),
            pltpu.VMEM((GROUPS, WIDE, COLS), BF16),
            pltpu.VMEM((GROUPS, TOGETHER, VDIM, RANK), BF16),
            pltpu.VMEM((BLOCK, WIDE), BF16),
            pltpu.VMEM((VT_ROWS, BLOCK), BF16),
            pltpu.VMEM((2, BLOCK, COLS), F32),
            pltpu.VMEM((GROUPS, VT_ROWS, COLS), F32),
            pltpu.VMEM((GROUPS, 8, COLS), F32),
            pltpu.SemaphoreType.DMA((SENDS,)),
            pltpu.SemaphoreType.DMA((RECEIVES,)),
            pltpu.SemaphoreType.DMA((LOCALS,)),
        ],
        compiler_params=pltpu.CompilerParams(
            collective_id=0, has_side_effects=True, vmem_limit_bytes=56 * 1024 * 1024
        ),
        cost_estimate=pl.CostEstimate(
            flops=13_000_000_000, bytes_accessed=6_000_000, transcendentals=5_000_000
        ),
    )(
        queries,
        latent.T,
        norm_gain.reshape(1, RANK),
        kv_up,
        block_mask,
        positions.reshape(1, ROWS),
    )


def solution(mesh):
    in_specs = (
        P(("blk", "kv"), None),
        P(("blk", "kv"), None),
        P(),
        P(),
        P("blk", None),
        P(("blk", "kv")),
    )
    return jax.shard_map(
        per_device, mesh=mesh, in_specs=in_specs, out_specs=P(("blk", "kv"), None), check_vma=False
    )
```
